512 devices in a mesh: ctx: 64 (over y, z), ch: 8 (over x, core).
Axes of the slice: x: 4, y: 4, z: 16, core: 2. Of those that a mesh axis runs over, the one named last changes fastest.
Arguments:
- query_rows: bfloat16 [8192, 8192], P('ctx', 'ch'), may hold values from -6 to 6
- key_rows: bfloat16 [8192, 8192], P('ctx', 'ch'), may hold values from -6 to 6
- value_rows: bfloat16 [8192, 8192], P('ctx', 'ch'), may hold values from -6 to 6
- short_filter: float32 [3, 3, 8192], P(None, None, 'ch'), may hold values from -3.5 to 3.5
- decay_rate: float32 [8192, 16], P('ch'), may hold values from 2e-05 to 0.1
- residues: float32 [8192, 16], P('ch'), may hold values from -1.5 to 1.5
- out_weight: bfloat16 [8192, 4096], P('ctx', 'ch'), may hold values from -0.1875 to 0.1875
- record_starts: int32 [4], replicated, may hold values from 0 to 8191, as said below
Outputs:
- block_out: bfloat16 [8192, 4096], P('ctx', 'ch')
The draws below stay inside these ranges and needn't reach their ends.
Inputs may be any that keep to these rules, and one draw needn't show every extreme that they name: record_starts[0] is 0 and the last entry is 8191; the entries are distinct and increasing, and all but the first lie in the second half of the 8192 tokens.
All inputs are finite; a program needn't handle non-finite values.
Results may differ from the reference program's by a relative error of at most 0.017.
Values may be sent and summed in bfloat16 or wider, within the bound.
A program may use at most 64 MiB of HBM per device.

```python
import math
import jax
import jax.numpy as jnp
from jax import lax

D = 8192
OUT = 4096
MODES = 16
KS = 3
NREC = 4
SEQ = 8192
N_CH = 8


def draw_record_starts(key, part):
    key = jax.random.fold_in(key, 17)
    halfway = SEQ // 2
    picks = jax.random.permutation(key, halfway - 1)[:NREC - 2] + halfway
    middle = jnp.sort(picks).astype(jnp.int32)
    first = jnp.zeros((1,), jnp.int32)
    last = jnp.full((1,), SEQ - 1, jnp.int32)
    return jnp.concatenate([first, middle, last])


def spiked(entries, rng, source, target, blocks, factor):
    owner, partner = [(jnp.arange(entries.shape[position]) // (entries.shape[position] // blocks)).reshape([-1 if axis == position else 1 for axis in range(entries.ndim)]) for position in (source, target)]
    chosen = jax.random.permutation(rng, blocks)[partner]
    strong = (owner == chosen) | (owner == (partner + blocks // 2) % blocks)
    return jnp.where(strong, factor * entries, entries)


def shard_levels(own_key, shape, cuts, smallest, largest):
    factor_of, own = 1.0, jax.random.fold_in(own_key, 6)
    for axis_at, parts in cuts:
        steps = jnp.exp(jax.random.uniform(jax.random.fold_in(own, axis_at), (parts,), jnp.float32, smallest / len(cuts), largest / len(cuts)))
        factor_of = factor_of * jnp.repeat(steps, shape[axis_at] // parts).reshape([-1 if axis == axis_at else 1 for axis in range(len(shape))])
    return factor_of


def centred(key, extent, width, reach, shards=(), kind=jnp.bfloat16):
    result = jax.random.normal(key, extent, jnp.float32) * width
    if len(shards) > 0:
        result = shard_levels(key, extent, shards, -0.22, 0.18) * result
    return jnp.clip(result, min=-reach, max=reach).astype(kind)


def bell_draw_with(own_key, extent, spread, bound, pieces, heavy, kind=jnp.bfloat16):
    drawn = spread * jax.random.normal(own_key, extent, jnp.float32)
    if pieces:
        drawn = drawn * shard_levels(own_key, extent, pieces, -0.22, 0.18)
    return jnp.clip(spiked(drawn, jax.random.fold_in(own_key, 3), *heavy), -bound, bound).astype(kind)


def setup_inputs(seed: int = 0) -> dict:
    key_of = jax.random.split(jax.random.key(seed), 9)
    return {
        "query_rows": centred(key_of[0], (SEQ, D), 1.0, 6.0, ((0, 64), (1, 8))),
        "key_rows": centred(key_of[1], (SEQ, D), 1.0, 6.0, ((0, 64), (1, 8))),
        "value_rows": centred(key_of[2], (SEQ, D), 1.0, 6.0, ((0, 64), (1, 8))),
        "short_filter": centred(key_of[3], (3, KS, D), KS ** -0.5, 3.5, ((2, 8),), jnp.float32),
        "decay_rate": jnp.clip(jnp.exp(math.log(0.1) - 8.517193 * jax.random.uniform(key_of[4], (D, MODES), jnp.float32) ** shard_levels(key_of[4], (D, MODES), ((0, 8),), -0.2, 0.2)), 1.9999999494757503e-05, 0.1),
        "residues": centred(key_of[5], (D, MODES), MODES ** -0.5, 1.5, ((0, 8),), jnp.float32),
        "out_weight": bell_draw_with(key_of[6], (D, OUT), D ** -0.5, 0.1875, ((0, 64), (1, 8)), (0, 1, 64, 4.0)),
        "record_starts": draw_record_starts(jax.random.fold_in(key_of[8], 71), 0),
    }


def ages_of(positions, record_starts):
    earlier = record_starts[None, :] <= positions[:, None]
    segment = lax.optimization_barrier(jnp.max(jnp.where(earlier, record_starts[None, :], 0), axis=1))
    return positions - segment

def masked_conv(extended, weights, ages, count):
    taps = weights.shape[0]
    total = jnp.zeros((count, extended.shape[1]), jnp.float32)
    for tap_index in range(taps):
        keeper = (ages >= tap_index).astype(jnp.float32)[:, None]
        window = extended[taps - 1 - tap_index:taps - 1 - tap_index + count]
        total = total + weights[tap_index][None, :] * window * keeper
    return total

def reference(query_rows, key_rows, value_rows, short_filter, decay_rate, residues, out_weight, record_starts):
    length = query_rows.shape[0]
    channels = D // N_CH
    positions = jnp.arange(length, dtype=jnp.int32)
    ages = ages_of(positions, record_starts)
    restart = jnp.any(record_starts[None, :] == positions[:, None], axis=1)
    kept_rows = 1.0 - restart.astype(jnp.float32)

    def split_rows(array):
        return jnp.transpose(array.reshape(length, N_CH, channels), (1, 0, 2))

    def padded(array, extra):
        return jnp.concatenate([jnp.zeros((extra, channels), jnp.float32), array.astype(jnp.float32)], axis=0)

    def one_block(inputs):
        query_blk, key_blk, value_blk, short_blk, rate_blk, residue_blk = inputs
        query_conv = masked_conv(padded(query_blk, KS - 1), short_blk[0], ages, length)
        key_conv = masked_conv(padded(key_blk, KS - 1), short_blk[1], ages, length)
        value_conv = masked_conv(padded(value_blk, KS - 1), short_blk[2], ages, length)
        mixed = (key_conv * value_conv).astype(jnp.bfloat16).astype(jnp.float32)
        decay = jnp.exp(-rate_blk)
        gain = jnp.sqrt(1.0 - jnp.exp(-2.0 * rate_blk))

        def advance(state, pair):
            row_values, kept = pair
            state = decay * state * kept + gain * row_values[:, None]
            return (state, lax.optimization_barrier(jnp.sum(residue_blk * state, axis=1)))
        init_state = jnp.zeros((channels, MODES), jnp.float32)
        unused, filtered = lax.scan(advance, init_state, (mixed, kept_rows))
        return (query_conv * filtered).astype(jnp.bfloat16)
    short_split = jnp.transpose(short_filter.reshape(3, KS, N_CH, channels), (2, 0, 1, 3))
    rate_split = decay_rate.reshape(N_CH, channels, MODES)
    residue_split = residues.reshape(N_CH, channels, MODES)
    gated_blocks = lax.map(one_block, (split_rows(query_rows), split_rows(key_rows), split_rows(value_rows), short_split, rate_split, residue_split))
    gated = jnp.transpose(gated_blocks, (1, 0, 2)).reshape(length, D)
    return jnp.dot(gated, out_weight, preferred_element_type=jnp.float32).astype(jnp.bfloat16)
```

```python
import functools

import jax
import jax.numpy as jnp
from jax import lax
from jax.experimental import pallas as pl
from jax.experimental.pallas import tpu as pltpu
from jax.sharding import PartitionSpec as P

MODES = 16
KS = 3
NX, NY, NZ, NC = 4, 4, 16, 2
TOK = 128
CH = 1024
G = CH // 128
COLS = 512
HALF = TOK // 2
MESH = pl.DeviceIdType.MESH
F32 = jnp.float32
BF16 = jnp.bfloat16


def exp_small(r):
    out = jnp.full_like(r, 1.0 / 5040.0)
    for c in (1.0 / 720.0, 1.0 / 120.0, 1.0 / 24.0, 1.0 / 6.0, 0.5, 1.0):
        out = c - r * out
    return 1.0 - r * out


def one_minus_exp(u):
    out = jnp.full_like(u, 1.0 / 40320.0)
    for c in (1.0 / 5040.0, 1.0 / 720.0, 1.0 / 120.0, 1.0 / 24.0, 1.0 / 6.0, 0.5, 1.0):
        out = c - u * out
    return u * out


def tree(parts):
    while len(parts) > 1:
        parts = [
            parts[i] + parts[i + 1] if i + 1 < len(parts) else parts[i]
            for i in range(0, len(parts), 2)
        ]
    return parts[0]


def kernel(
    q_in, k_in, v_in, sf_in, rate_in, res_in, w_in, rs,
    out_ref,
    q_raw, k_raw, v_raw, qt, kt, vt, xt, yt, gt, sft, ratet, rest, lamt, wt,
    fin, got, ebuf, rbuf, rgot, gref, ent, wbuf, abuf, pbuf, qbuf, rsum,
    load_sem, halo_send, halo_recv, tr_sem, wsend, wrecv,
    s1_send, s1_recv, s2_send, s2_recv, s3_send, s3_recv,
    a_send, a_recv, sib_send, sib_recv, c_send, c_recv, x_send, x_recv,
):
    ctx = lax.axis_index("ctx")
    ch = lax.axis_index("ch")
    y, z = ctx // NZ, lax.rem(ctx, NZ)
    x, c = ch // NC, lax.rem(ch, NC)

    def dev(xx, cc, yy, zz):
        return (yy * NZ + zz, xx * NC + cc)

    def zpeer(d):
        return lax.rem(z + d, NZ)

    def ypeer(d):
        return lax.rem(y + d, NY)

    def xpeer(d):
        return lax.rem(x + d, NX)

    n_ctx = NY * NZ
    after = (lax.rem(ctx + 1, n_ctx), ch)
    before = (lax.rem(ctx + n_ctx - 1, n_ctx), ch)
    sibling = dev(x, 1 - c, y, z)
    flipped = dev(y, c, x, z)

    barrier = pltpu.get_barrier_semaphore()

    def greet(d):
        pl.semaphore_signal(barrier, inc=1, device_id=d, device_id_type=MESH)

    for d in range(1, NZ):
        greet(dev(x, c, y, zpeer(d)))
    for d in range(1, NY):
        greet(dev(x, c, ypeer(d), z))
    for d in range(1, NX):
        greet(dev(xpeer(d), c, y, z))
    greet(sibling)
    greet(before)
    greet(after)

    @pl.when(x != y)
    def _():
        greet(flipped)

    loads = [
        pltpu.make_async_copy(src, dst, load_sem.at[i])
        for i, (src, dst) in enumerate(((k_in, k_raw), (v_in, v_raw), (q_in, q_raw)))
    ]
    for load in loads:
        load.start()

    for g in range(G):
        lanes = slice(g * 128, (g + 1) * 128)
        ratet[pl.ds(g, MODES, stride=G), :] = rate_in[:, lanes]
        rest[pl.ds(g, MODES, stride=G), :] = res_in[:, lanes]
        for i in range(3):
            sft[pl.ds(i * KS * G + g, KS, stride=G), :] = sf_in[i, :, lanes]
    rate_all = ratet[...]
    lamt[...] = exp_small(rate_all)
    wt[...] = rest[...] * jnp.sqrt(one_minus_exp(2.0 * rate_all))

    def spread(raw, dst):
        for g in range(G):
            lanes = slice(g * 128, (g + 1) * 128)
            dst[pl.ds(2 * G + g, TOK, stride=G), :] = raw[:, lanes].astype(F32)

    loads[0].wait()
    spread(k_raw, kt)
    loads[1].wait()
    spread(v_raw, vt)
    loads[2].wait()
    spread(q_raw, qt)

    partners = (NZ - 1) + (NY - 1) + (NX - 1) + 3 + jnp.where(x != y, 1, 0)
    pl.semaphore_wait(barrier, partners)

    halos = []
    for i, arr in enumerate((kt, vt, qt)):
        halos.append(
            pltpu.make_async_remote_copy(
                src_ref=arr.at[pl.ds(TOK * G, 2 * G), :],
                dst_ref=arr.at[pl.ds(0, 2 * G), :],
                send_sem=halo_send.at[i],
                recv_sem=halo_recv.at[i],
                device_id=after,
                device_id_type=MESH,
            )
        )

    def wslot(s):
        return wbuf.at[pl.ds(pl.multiple_of(s * TOK, TOK), TOK), :]

    def wpart(s, first, count):
        return wbuf.at[pl.ds(pl.multiple_of(s * TOK + first, HALF), count), :]

    flip = pltpu.make_async_remote_copy(
        src_ref=w_in,
        dst_ref=wslot(z),
        send_sem=tr_sem.at[0],
        recv_sem=tr_sem.at[1],
        device_id=flipped,
        device_id_type=MESH,
    )
    keep_w = pltpu.make_async_copy(w_in, wslot(z), tr_sem.at[2])

    @pl.when(x != y)
    def _():
        flip.start()

    @pl.when(x == y)
    def _():
        keep_w.start()

    for h in halos:
        h.start()

    def wcopy(s, right):
        first, count = 0, TOK
        if s == NZ // 2 - 1:
            first, count = (0, HALF) if right else (HALF, HALF)
        slot = lax.rem(z + NZ - s, NZ) if right else lax.rem(z + s, NZ)
        side = 0 if right else 1
        return pltpu.make_async_remote_copy(
            src_ref=wpart(slot, first, count),
            dst_ref=wpart(slot, first, count),
            send_sem=wsend.at[side, s],
            recv_sem=wrecv.at[side, s],
            device_id=dev(x, c, y, zpeer(1 if right else NZ - 1)),
            device_id_type=MESH,
        )

    def w_step(s):
        if s == 0:
            @pl.when(x != y)
            def _():
                flip.wait_recv()

            @pl.when(x == y)
            def _():
                keep_w.wait()
        else:
            wcopy(s - 1, True).wait_recv()
            wcopy(s - 1, False).wait_recv()
        if s < NZ // 2:
            wcopy(s, True).start()
            wcopy(s, False).start()

    base = ctx * TOK
    starts = [rs[i] for i in range(4)]

    def seg_of(pos):
        seg = jnp.int32(0)
        for st in starts:
            seg = jnp.maximum(seg, jnp.where(st <= pos, st, 0))
        return seg

    def tile(ref, t):
        return ref[pl.ds(pl.multiple_of(t * G, G), G), :]

    def put(ref, t, val):
        ref[pl.ds(pl.multiple_of(t * G, G), G), :] = val

    def age_masks(pos):
        age = pos - seg_of(pos)
        return jnp.where(age >= 1, 1.0, 0.0).astype(F32), jnp.where(age >= 2, 1.0, 0.0).astype(F32)

    def taps(i):
        return [sft[(i * KS + j) * G : (i * KS + j + 1) * G, :] for j in range(KS)]

    def conv(ref, w, t, m1, m2):
        return w[0] * tile(ref, t + 2) + w[1] * tile(ref, t + 1) * m1 + w[2] * tile(ref, t) * m2

    def mix(t):
        m1, m2 = age_masks(base + t)
        return (conv(kt, taps(1), t, m1, m2) * conv(vt, taps(2), t, m1, m2)).astype(BF16).astype(F32)

    lams = lambda: [lamt[m * G : (m + 1) * G, :] for m in range(MODES)]
    ws = lambda: [wt[m * G : (m + 1) * G, :] for m in range(MODES)]
    last_seg = seg_of(base + TOK - 1)

    def pass1(i, state):
        lam = lams()
        for u in range(6):
            t = 2 + i * 6 + u
            val = mix(t)
            put(xt, t, val)
            val = val * jnp.where(base + t >= last_seg, 1.0, 0.0).astype(F32)
            state = [s * l + val for s, l in zip(state, lam)]
        return state

    zero = jnp.zeros((G, 128), F32)
    state = lax.fori_loop(0, (TOK - 2) // 6, pass1, [zero] * MODES)
    w_step(0)
    halos[0].wait_recv()
    halos[1].wait_recv()
    val0, val1 = mix(0), mix(1)
    put(xt, 0, val0)
    put(xt, 1, val1)
    val0 = val0 * jnp.where(base >= last_seg, 1.0, 0.0).astype(F32)
    val1 = val1 * jnp.where(base + 1 >= last_seg, 1.0, 0.0).astype(F32)
    for m in range(MODES):
        rows = slice(m * G, (m + 1) * G)
        far = jnp.exp(ratet[rows, :] * (-(TOK - 2.0)))
        fin[rows, :] = state[m] + far * (lamt[rows, :] * val0 + val1)

    def zexchange(src, dst, send, recv):
        def one(d):
            peer = zpeer(d)
            return pltpu.make_async_remote_copy(
                src_ref=src.at[pl.ds(pl.multiple_of(peer * G, G), G), :],
                dst_ref=dst.at[pl.ds(pl.multiple_of(z * G, G), G), :],
                send_sem=send.at[d],
                recv_sem=recv.at[d],
                device_id=dev(x, c, y, peer),
                device_id_type=MESH,
            )

        return [one(d) for d in range(1, NZ)]

    to_mode = zexchange(fin, got, s1_send, s1_recv)
    for cp in to_mode:
        cp.start()
    put(got, z, tile(fin, z))

    halos[2].wait_recv()

    def qconv(i, carry):
        for u in range(8):
            t = i * 8 + u
            m1, m2 = age_masks(base + t)
            put(gt, t, conv(qt, taps(0), t, m1, m2))
        return carry

    def local_part(i, state):
        lam, w = lams(), ws()
        for u in range(8):
            t = i * 8 + u
            val = tile(xt, t)
            m1, _ = age_masks(base + t)
            state = [s * m1 * l + val for s, l in zip(state, lam)]
            put(yt, t, tree([a * b for a, b in zip(w, state)]))
        return state

    lax.fori_loop(0, TOK // 8, qconv, 0)
    w_step(1)
    state = lax.fori_loop(0, TOK // 16, local_part, [zero] * MODES)

    def unbroken(first, count):
        hit = jnp.int32(0)
        for st in starts:
            hit = hit + jnp.where((st >= first) & (st < first + count), 1, 0)
        return jnp.where(hit == 0, 1.0, 0.0).astype(F32)

    for cp in to_mode:
        cp.wait_recv()
    rate_m = tile(ratet, z)
    one_block = jnp.exp(rate_m * (-float(TOK)))
    one_row = jnp.exp(rate_m * (-float(TOK * NZ)))
    entry = zero
    for zz in range(NZ):
        ebuf[zz * G : (zz + 1) * G, :] = entry
        entry = entry * (one_block * unbroken((y * NZ + zz) * TOK, TOK)) + got[zz * G : (zz + 1) * G, :]
    rbuf[...] = entry

    to_rows = [
        pltpu.make_async_remote_copy(
            src_ref=rbuf,
            dst_ref=rgot.at[pl.ds(pl.multiple_of(y * G, G), G), :],
            send_sem=s2_send.at[d],
            recv_sem=s2_recv.at[d],
            device_id=dev(x, c, ypeer(d), z),
            device_id_type=MESH,
        )
        for d in range(1, NY)
    ]
    for cp in to_rows:
        cp.start()
    state = lax.fori_loop(TOK // 16, TOK // 8, local_part, state)
    w_step(2)
    for cp in to_rows:
        cp.wait_recv()
    gref[...] = zero
    for yy in range(NY - 1):
        @pl.when(yy < y)
        def _():
            gref[...] = gref[...] * (one_row * unbroken(yy * NZ * TOK, NZ * TOK)) + rgot[yy * G : (yy + 1) * G, :]

    entry = gref[...]
    for zz in range(NZ):
        rows = slice(zz * G, (zz + 1) * G)
        ebuf[rows, :] = ebuf[rows, :] + entry
        entry = entry * (one_block * unbroken((y * NZ + zz) * TOK, TOK))
    to_back = zexchange(ebuf, ent, s3_send, s3_recv)
    for cp in to_back:
        cp.start()
    put(ent, z, tile(ebuf, z))
    for cp in to_back:
        cp.wait_recv()

    def correct(i, state):
        lam = lams()
        for u in range(8):
            t = i * 8 + u
            free = jnp.where(seg_of(base + t) < base, 1.0, 0.0).astype(F32)
            filtered = tile(yt, t) + tree(list(state)) * free
            put(gt, t, tile(gt, t) * filtered)
            state = [s * l for s, l in zip(state, lam)]
        return state

    init = []
    for m in range(MODES):
        rows = slice(m * G, (m + 1) * G)
        init.append(ent[rows, :] * lamt[rows, :] * wt[rows, :])
    state = init

    def ablock(yy, cc, h):
        return abuf.at[yy, cc, pl.ds(h * HALF, HALF), :]

    def acopy(yy, h, right, index):
        return pltpu.make_async_remote_copy(
            src_ref=ablock(yy, c, h),
            dst_ref=ablock(yy, c, h),
            send_sem=a_send.at[index],
            recv_sem=a_recv.at[index],
            device_id=dev(x, c, ypeer(1 if right else NY - 1), z),
            device_id_type=MESH,
        )

    def sibcopy(d, h):
        yy = ypeer(d)
        return pltpu.make_async_remote_copy(
            src_ref=ablock(yy, c, h),
            dst_ref=ablock(yy, c, h),
            send_sem=sib_send.at[d, h],
            recv_sem=sib_recv.at[d, h],
            device_id=sibling,
            device_id_type=MESH,
        )

    for h in range(2):
        state = lax.fori_loop(h * (TOK // 16), (h + 1) * (TOK // 16), correct, state)
        for g in range(G):
            part = gt[pl.ds(h * HALF * G + g, HALF, stride=G), :].astype(BF16)
            abuf[y, c, h * HALF : (h + 1) * HALF, g * 128 : (g + 1) * 128] = part
        acopy(y, h, True, h).start()
        acopy(y, h, False, 2 + h).start()
        sibcopy(0, h).start()

    w_step(3)
    left, right, far = ypeer(NY - 1), ypeer(1), ypeer(2)
    acopy(y, 0, True, 0).wait_recv()
    acopy(left, 0, True, 4).start()
    sibcopy(3, 0).start()
    acopy(y, 0, False, 2).wait_recv()
    sibcopy(1, 0).start()
    w_step(4)
    acopy(y, 1, False, 3).wait_recv()
    acopy(right, 1, False, 5).start()
    sibcopy(1, 1).start()
    acopy(y, 1, True, 1).wait_recv()
    sibcopy(3, 1).start()
    w_step(5)
    acopy(far, 0, True, 4).wait_recv()
    sibcopy(2, 0).start()
    w_step(6)
    acopy(far, 1, False, 5).wait_recv()
    sibcopy(2, 1).start()
    w_step(7)
    w_step(8)

    def product(yy):
        acc = jnp.dot(abuf[yy, 0], wbuf[0:CH, :], preferred_element_type=F32)
        return acc + jnp.dot(abuf[yy, 1], wbuf[CH : 2 * CH, :], preferred_element_type=F32)

    def ccopy(d):
        return pltpu.make_async_remote_copy(
            src_ref=pbuf.at[d],
            dst_ref=qbuf.at[y],
            send_sem=c_send.at[d],
            recv_sem=c_recv.at[d],
            device_id=dev(x, c, ypeer(d), z),
            device_id_type=MESH,
        )

    def xcopy(o, d):
        return pltpu.make_async_remote_copy(
            src_ref=qbuf.at[o],
            dst_ref=rsum.at[x],
            send_sem=x_send.at[d],
            recv_sem=x_recv.at[d],
            device_id=dev(o, c, y, z),
            device_id_type=MESH,
        )

    def pass_on(o):
        for d in range(1, NX):
            @pl.when(o == xpeer(d))
            def _():
                xcopy(xpeer(d), d).start()

        @pl.when(o == x)
        def _():
            rsum[x] = qbuf[o]

    for d in (2, 1, 3, 0):
        for h in range(2):
            sibcopy(d, h).wait_recv()
        res = product(ypeer(d)).astype(BF16)
        if d == 0:
            qbuf[y] = res
            pass_on(y)
        else:
            pbuf[d] = res
            ccopy(d).start()
    for d in (3, 1, 2):
        ccopy(d).wait_recv()
        pass_on(ypeer(NY - d))
    for d in range(1, NX):
        xcopy(xpeer(d), d).wait_recv()
    total = rsum[0].astype(F32) + rsum[1].astype(F32) + rsum[2].astype(F32) + rsum[3].astype(F32)
    out_ref[...] = total.astype(BF16)

    @pl.when(x != y)
    def _():
        flip.wait_send()

    for h in halos:
        h.wait_send()
    for s in range(NZ // 2):
        wcopy(s, True).wait_send()
        wcopy(s, False).wait_send()
    for cp in to_mode + to_rows + to_back:
        cp.wait_send()
    for h in range(2):
        acopy(y, h, True, h).wait_send()
        acopy(y, h, False, 2 + h).wait_send()
    acopy(left, 0, True, 4).wait_send()
    acopy(right, 1, False, 5).wait_send()
    for d in range(NY):
        for h in range(2):
            sibcopy(d, h).wait_send()
    for d in range(1, NY):
        ccopy(d).wait_send()
    for d in range(1, NX):
        xcopy(xpeer(d), d).wait_send()


def local(
    query_rows, key_rows, value_rows, short_filter, decay_rate, residues, out_weight, record_starts
):
    vmem = pl.BlockSpec(memory_space=pltpu.VMEM)
    hbm = pl.BlockSpec(memory_space=pl.ANY)
    smem = pl.BlockSpec(memory_space=pltpu.SMEM)
    tokens = pltpu.VMEM((TOK * G, 128), F32)
    longer = pltpu.VMEM(((TOK + 2) * G, 128), F32)
    table = pltpu.VMEM((MODES * G, 128), F32)
    dma = pltpu.SemaphoreType.DMA
    return pl.pallas_call(
        kernel,
        out_shape=jax.ShapeDtypeStruct((TOK, COLS), BF16),
        in_specs=[hbm, hbm, hbm, vmem, vmem, vmem, hbm, smem],
        out_specs=vmem,
        scratch_shapes=[
            pltpu.VMEM((TOK, CH), BF16), pltpu.VMEM((TOK, CH), BF16), pltpu.VMEM((TOK, CH), BF16),
            longer, longer, longer, tokens, tokens, tokens,
            pltpu.VMEM((9 * G, 128), F32), table, table, table, table,
            table, table, table, pltpu.VMEM((G, 128), F32), pltpu.VMEM((NY * G, 128), F32),
            pltpu.VMEM((G, 128), F32), table,
            pltpu.VMEM((NZ * TOK, COLS), BF16),
            pltpu.VMEM((NY, NC, TOK, CH), BF16),
            pltpu.VMEM((NY, TOK, COLS), BF16),
            pltpu.VMEM((NY, TOK, COLS), BF16),
            pltpu.VMEM((NX, TOK, COLS), BF16),
            dma((3,)), dma((3,)), dma((3,)), dma((3,)), dma((2, 8)), dma((2, 8)),
            dma((NZ,)), dma((NZ,)), dma((NY,)), dma((NY,)), dma((NZ,)), dma((NZ,)),
            dma((6,)), dma((6,)), dma((NY, 2)), dma((NY, 2)),
            dma((NY,)), dma((NY,)), dma((NX,)), dma((NX,)),
        ],
        compiler_params=pltpu.CompilerParams(
            collective_id=0, has_side_effects=True, vmem_limit_bytes=40 * 1024 * 1024
        ),
    )(
        query_rows, key_rows, value_rows, short_filter,
        decay_rate.T, residues.T, out_weight, record_starts,
    )


def solution(mesh):
    return jax.shard_map(
        local,
        mesh=mesh,
        in_specs=(
            P("ctx", "ch"),
            P("ctx", "ch"),
            P("ctx", "ch"),
            P(None, None, "ch"),
            P("ch", None),
            P("ch", None),
            P("ctx", "ch"),
            P(),
        ),
        out_specs=P("ctx", "ch"),
        check_vma=False,
    )
```

```python
import functools

import jax
import jax.numpy as jnp
from jax import lax
from jax.experimental import pallas as pl
from jax.experimental.pallas import tpu as pltpu
from jax.sharding import PartitionSpec as P

MODES = 16
KS = 3
NX, NY, NZ, NC = 4, 4, 16, 2
TOK = 128
CH = 1024
G = CH // 128
COLS = 512
HALF = TOK // 2
PIECES = 4
PIECE = TOK // PIECES
MESH = pl.DeviceIdType.MESH
F32 = jnp.float32
BF16 = jnp.bfloat16


def exp_small(r):
    out = jnp.full_like(r, 1.0 / 5040.0)
    for c in (1.0 / 720.0, 1.0 / 120.0, 1.0 / 24.0, 1.0 / 6.0, 0.5, 1.0):
        out = c - r * out
    return 1.0 - r * out


def one_minus_exp(u):
    out = jnp.full_like(u, 1.0 / 40320.0)
    for c in (1.0 / 5040.0, 1.0 / 720.0, 1.0 / 120.0, 1.0 / 24.0, 1.0 / 6.0, 0.5, 1.0):
        out = c - u * out
    return u * out


def tree(parts):
    while len(parts) > 1:
        parts = [
            parts[i] + parts[i + 1] if i + 1 < len(parts) else parts[i]
            for i in range(0, len(parts), 2)
        ]
    return parts[0]


def kernel(
    q_in, k_in, v_in, sf_hbm, rate_hbm, res_hbm, w_in, rs,
    out_ref,
    q_raw, k_raw, v_raw, sf_in, rate_in, res_in, qt, kt, vt, xt, yt, gt, sft, ratet, rest, lamt, wt,
    fin, got, ebuf, rbuf, rgot, gref, ent, wbuf, abuf, pbuf, qbuf, rsum,
    load_sem, halo_send, halo_recv, tr_sem, keep_sem, wsend, wrecv,
    s1_send, s1_recv, s2_send, s2_recv, s3_send, s3_recv,
    a_send, a_recv, sib_send, sib_recv, c_send, c_recv, x_send, x_recv,
):
    ctx = lax.axis_index("ctx")
    ch = lax.axis_index("ch")
    y, z = ctx // NZ, lax.rem(ctx, NZ)
    x, c = ch // NC, lax.rem(ch, NC)

    def dev(xx, cc, yy, zz):
        return (yy * NZ + zz, xx * NC + cc)

    def zpeer(d):
        return lax.rem(z + d, NZ)

    def ypeer(d):
        return lax.rem(y + d, NY)

    def xpeer(d):
        return lax.rem(x + d, NX)

    n_ctx = NY * NZ
    after = (lax.rem(ctx + 1, n_ctx), ch)
    before = (lax.rem(ctx + n_ctx - 1, n_ctx), ch)
    sibling = dev(x, 1 - c, y, z)
    flipped = dev(y, c, x, z)

    loads = [
        pltpu.make_async_copy(src, dst, load_sem.at[i])
        for i, (src, dst) in enumerate(
            (
                (k_in, k_raw), (v_in, v_raw), (q_in, q_raw),
                (rate_hbm, rate_in), (res_hbm, res_in), (sf_hbm, sf_in),
            )
        )
    ]
    for load in loads:
        load.start()

    barrier = pltpu.get_barrier_semaphore()

    def greet(d):
        pl.semaphore_signal(barrier, inc=1, device_id=d, device_id_type=MESH)

    for d in range(1, NZ):
        greet(dev(x, c, y, zpeer(d)))
    for d in range(1, NY):
        greet(dev(x, c, ypeer(d), z))
    for d in range(1, NX):
        greet(dev(xpeer(d), c, y, z))
    greet(sibling)
    greet(before)
    greet(after)

    @pl.when(x != y)
    def _():
        greet(flipped)

    partners = (NZ - 1) + (NY - 1) + (NX - 1) + 3 + jnp.where(x != y, 1, 0)
    pl.semaphore_wait(barrier, partners)

    halos = []
    for i, arr in enumerate((kt, vt, qt)):
        halos.append(
            pltpu.make_async_remote_copy(
                src_ref=arr.at[pl.ds(TOK * G, 2 * G), :],
                dst_ref=arr.at[pl.ds(0, 2 * G), :],
                send_sem=halo_send.at[i],
                recv_sem=halo_recv.at[i],
                device_id=after,
                device_id_type=MESH,
            )
        )

    def wslot(s):
        return wbuf.at[pl.ds(pl.multiple_of(s * TOK, TOK), TOK), :]

    def wpart(s, first, count):
        return wbuf.at[pl.ds(pl.multiple_of(s * TOK + first, PIECE), count), :]

    def flip(k):
        return pltpu.make_async_remote_copy(
            src_ref=w_in.at[pl.ds(k * PIECE, PIECE), :],
            dst_ref=wpart(z, k * PIECE, PIECE),
            send_sem=tr_sem.at[0, k],
            recv_sem=tr_sem.at[1, k],
            device_id=flipped,
            device_id_type=MESH,
        )

    keep_w = pltpu.make_async_copy(w_in, wslot(z), keep_sem.at[0])

    @pl.when(x != y)
    def _():
        for k in range(PIECES):
            flip(k).start()

    @pl.when(x == y)
    def _():
        keep_w.start()

    def spread(raw, dst, first, count):
        for g in range(G):
            lanes = slice(g * 128, (g + 1) * 128)
            dst[pl.ds((2 + first) * G + g, count, stride=G), :] = raw[first : first + count, lanes].astype(F32)

    for i, (raw, dst) in enumerate(((k_raw, kt), (v_raw, vt))):
        loads[i].wait()
        spread(raw, dst, TOK - 16, 16)
        halos[i].start()

    for load in loads[3:]:
        load.wait()
    for g in range(G):
        lanes = slice(g * 128, (g + 1) * 128)
        ratet[pl.ds(g, MODES, stride=G), :] = rate_in[:, lanes]
        rest[pl.ds(g, MODES, stride=G), :] = res_in[:, lanes]
        for i in range(3):
            sft[pl.ds(i * KS * G + g, KS, stride=G), :] = sf_in[i, :, lanes]
    rate_all = ratet[...]
    lamt[...] = exp_small(rate_all)
    wt[...] = rest[...] * jnp.sqrt(one_minus_exp(2.0 * rate_all))

    spread(k_raw, kt, 0, TOK - 16)
    spread(v_raw, vt, 0, TOK - 16)
    loads[2].wait()
    spread(q_raw, qt, TOK - 16, 16)
    halos[2].start()
    spread(q_raw, qt, 0, TOK - 16)

    STEPS = NZ // 2

    def wcopy(n, right):
        hop, part = n // PIECES, n % PIECES
        slot = lax.rem(z + NZ - hop, NZ) if right else lax.rem(z + hop, NZ)
        side = 0 if right else 1
        return pltpu.make_async_remote_copy(
            src_ref=wpart(slot, part * PIECE, PIECE),
            dst_ref=wpart(slot, part * PIECE, PIECE),
            send_sem=wsend.at[side, n],
            recv_sem=wrecv.at[side, n],
            device_id=dev(x, c, y, zpeer(1 if right else NZ - 1)),
            device_id_type=MESH,
        )

    def w_goes(n, right):
        return n < PIECES * STEPS and (n // PIECES < STEPS - 1 or (n % 2 == 0) == right)

    def w_step(n):
        if n < PIECES:
            @pl.when(x != y)
            def _():
                flip(n).wait_recv()

            if n == 0:
                @pl.when(x == y)
                def _():
                    keep_w.wait()

        for right in (True, False):
            if n >= PIECES and w_goes(n - PIECES, right):
                wcopy(n - PIECES, right).wait_recv()
            if w_goes(n, right):
                wcopy(n, right).start()

    def w_hop(h):
        for part in range(PIECES):
            w_step(h * PIECES + part)

    base = ctx * TOK
    starts = [rs[i] for i in range(4)]

    def seg_of(pos):
        seg = jnp.int32(0)
        for st in starts:
            seg = jnp.maximum(seg, jnp.where(st <= pos, st, 0))
        return seg

    def tile(ref, t):
        return ref[pl.ds(pl.multiple_of(t * G, G), G), :]

    def put(ref, t, val):
        ref[pl.ds(pl.multiple_of(t * G, G), G), :] = val

    def age_masks(pos):
        age = pos - seg_of(pos)
        return jnp.where(age >= 1, 1.0, 0.0).astype(F32), jnp.where(age >= 2, 1.0, 0.0).astype(F32)

    def taps(i):
        return [sft[(i * KS + j) * G : (i * KS + j + 1) * G, :] for j in range(KS)]

    def conv(ref, w, t, m1, m2):
        return w[0] * tile(ref, t + 2) + w[1] * tile(ref, t + 1) * m1 + w[2] * tile(ref, t) * m2

    def mix(t):
        m1, m2 = age_masks(base + t)
        return (conv(kt, taps(1), t, m1, m2) * conv(vt, taps(2), t, m1, m2)).astype(BF16).astype(F32)

    lams = lambda: [lamt[m * G : (m + 1) * G, :] for m in range(MODES)]
    ws = lambda: [wt[m * G : (m + 1) * G, :] for m in range(MODES)]
    last_seg = seg_of(base + TOK - 1)

    def pass1(i, state):
        lam = lams()
        for u in range(6):
            t = 2 + i * 6 + u
            val = mix(t)
            put(xt, t, val)
            val = val * jnp.where(base + t >= last_seg, 1.0, 0.0).astype(F32)
            state = [s * l + val for s, l in zip(state, lam)]
        return state

    zero = jnp.zeros((G, 128), F32)
    state = lax.fori_loop(0, (TOK - 2) // 6, pass1, [zero] * MODES)
    halos[0].wait_recv()
    halos[1].wait_recv()
    val0, val1 = mix(0), mix(1)
    put(xt, 0, val0)
    put(xt, 1, val1)
    val0 = val0 * jnp.where(base >= last_seg, 1.0, 0.0).astype(F32)
    val1 = val1 * jnp.where(base + 1 >= last_seg, 1.0, 0.0).astype(F32)
    for m in range(MODES):
        rows = slice(m * G, (m + 1) * G)
        far = jnp.exp(ratet[rows, :] * (-(TOK - 2.0)))
        fin[rows, :] = state[m] + far * (lamt[rows, :] * val0 + val1)

    def zexchange(src, dst, send, recv):
        def one(d):
            peer = zpeer(d)
            return pltpu.make_async_remote_copy(
                src_ref=src.at[pl.ds(pl.multiple_of(peer * G, G), G), :],
                dst_ref=dst.at[pl.ds(pl.multiple_of(z * G, G), G), :],
                send_sem=send.at[d],
                recv_sem=recv.at[d],
                device_id=dev(x, c, y, peer),
                device_id_type=MESH,
            )

        return [one(d) for d in range(1, NZ)]

    to_mode = zexchange(fin, got, s1_send, s1_recv)
    for cp in to_mode:
        cp.start()
    put(got, z, tile(fin, z))

    halos[2].wait_recv()

    def qconv(i, carry):
        for u in range(8):
            t = i * 8 + u
            m1, m2 = age_masks(base + t)
            put(gt, t, conv(qt, taps(0), t, m1, m2))
        return carry

    def local_part(i, state):
        lam, w = lams(), ws()
        for u in range(8):
            t = i * 8 + u
            val = tile(xt, t)
            m1, _ = age_masks(base + t)
            state = [s * m1 * l + val for s, l in zip(state, lam)]
            put(yt, t, tree([a * b for a, b in zip(w, state)]))
        return state

    lax.fori_loop(0, TOK // 8, qconv, 0)
    state = lax.fori_loop(0, TOK // 16, local_part, [zero] * MODES)
    w_hop(0)
    state = lax.fori_loop(TOK // 16, TOK // 8, local_part, state)
    w_hop(1)

    def unbroken(first, count):
        hit = jnp.int32(0)
        for st in starts:
            hit = hit + jnp.where((st >= first) & (st < first + count), 1, 0)
        return jnp.where(hit == 0, 1.0, 0.0).astype(F32)

    for cp in to_mode:
        cp.wait_recv()
    rate_m = tile(ratet, z)
    one_block = jnp.exp(rate_m * (-float(TOK)))
    one_row = jnp.exp(rate_m * (-float(TOK * NZ)))
    entry = zero
    for zz in range(NZ):
        ebuf[zz * G : (zz + 1) * G, :] = entry
        entry = entry * (one_block * unbroken((y * NZ + zz) * TOK, TOK)) + got[zz * G : (zz + 1) * G, :]
    rbuf[...] = entry

    to_rows = [
        pltpu.make_async_remote_copy(
            src_ref=rbuf,
            dst_ref=rgot.at[pl.ds(pl.multiple_of(y * G, G), G), :],
            send_sem=s2_send.at[d],
            recv_sem=s2_recv.at[d],
            device_id=dev(x, c, ypeer(d), z),
            device_id_type=MESH,
        )
        for d in range(1, NY)
    ]
    for cp in to_rows:
        cp.start()
    w_hop(2)
    for cp in to_rows:
        cp.wait_recv()
    gref[...] = zero
    for yy in range(NY - 1):
        @pl.when(yy < y)
        def _():
            gref[...] = gref[...] * (one_row * unbroken(yy * NZ * TOK, NZ * TOK)) + rgot[yy * G : (yy + 1) * G, :]

    entry = gref[...]
    for zz in range(NZ):
        rows = slice(zz * G, (zz + 1) * G)
        ebuf[rows, :] = ebuf[rows, :] + entry
        entry = entry * (one_block * unbroken((y * NZ + zz) * TOK, TOK))
    to_back = zexchange(ebuf, ent, s3_send, s3_recv)
    for cp in to_back:
        cp.start()
    put(ent, z, tile(ebuf, z))
    for hop in (3, 4, 5):
        w_hop(hop)
    for cp in to_back:
        cp.wait_recv()

    def correct(i, state):
        lam = lams()
        for u in range(8):
            t = i * 8 + u
            free = jnp.where(seg_of(base + t) < base, 1.0, 0.0).astype(F32)
            filtered = tile(yt, t) + tree(list(state)) * free
            put(gt, t, tile(gt, t) * filtered)
            state = [s * l for s, l in zip(state, lam)]
        return state

    init = []
    for m in range(MODES):
        rows = slice(m * G, (m + 1) * G)
        init.append(ent[rows, :] * lamt[rows, :] * wt[rows, :])
    state = init

    def ablock(yy, cc, h):
        return abuf.at[yy, cc, pl.ds(h * HALF, HALF), :]

    def acopy(yy, h, right, index):
        return pltpu.make_async_remote_copy(
            src_ref=ablock(yy, c, h),
            dst_ref=ablock(yy, c, h),
            send_sem=a_send.at[index],
            recv_sem=a_recv.at[index],
            device_id=dev(x, c, ypeer(1 if right else NY - 1), z),
            device_id_type=MESH,
        )

    def sibcopy(d, h):
        yy = ypeer(d)
        return pltpu.make_async_remote_copy(
            src_ref=ablock(yy, c, h),
            dst_ref=ablock(yy, c, h),
            send_sem=sib_send.at[d, h],
            recv_sem=sib_recv.at[d, h],
            device_id=sibling,
            device_id_type=MESH,
        )

    for h in range(2):
        state = lax.fori_loop(h * (TOK // 16), (h + 1) * (TOK // 16), correct, state)
        for g in range(G):
            part = gt[pl.ds(h * HALF * G + g, HALF, stride=G), :].astype(BF16)
            abuf[y, c, h * HALF : (h + 1) * HALF, g * 128 : (g + 1) * 128] = part
        if h == 1:
            acopy(y, 1, False, 3).start()
        acopy(y, h, True, h).start()
        sibcopy(0, h).start()
    acopy(y, 0, False, 2).start()

    lhs, rhs, far = ypeer(NY - 1), ypeer(1), ypeer(2)
    w_hop(6)
    acopy(y, 0, True, 0).wait_recv()
    acopy(lhs, 0, True, 4).start()
    sibcopy(3, 0).start()
    acopy(y, 1, False, 3).wait_recv()
    acopy(rhs, 1, False, 5).start()
    sibcopy(1, 1).start()
    w_hop(7)
    acopy(y, 1, True, 1).wait_recv()
    sibcopy(3, 1).start()
    acopy(y, 0, False, 2).wait_recv()
    sibcopy(1, 0).start()
    w_hop(8)

    def product(yy):
        acc = jnp.dot(abuf[yy, 0], wbuf[0:CH, :], preferred_element_type=F32)
        return acc + jnp.dot(abuf[yy, 1], wbuf[CH : 2 * CH, :], preferred_element_type=F32)

    def ccopy(d):
        return pltpu.make_async_remote_copy(
            src_ref=pbuf.at[d],
            dst_ref=qbuf.at[y],
            send_sem=c_send.at[d],
            recv_sem=c_recv.at[d],
            device_id=dev(x, c, ypeer(d), z),
            device_id_type=MESH,
        )

    def xcopy(o, d):
        return pltpu.make_async_remote_copy(
            src_ref=qbuf.at[o],
            dst_ref=rsum.at[x],
            send_sem=x_send.at[d],
            recv_sem=x_recv.at[d],
            device_id=dev(o, c, y, z),
            device_id_type=MESH,
        )

    def pass_on(o):
        for d in range(1, NX):
            @pl.when(o == xpeer(d))
            def _():
                xcopy(xpeer(d), d).start()

        @pl.when(o == x)
        def _():
            rsum[x] = qbuf[o]

    def send_product(d):
        for h in range(2):
            sibcopy(d, h).wait_recv()
        part = product(ypeer(d)).astype(BF16)
        if d == 0:
            qbuf[y] = part
            pass_on(y)
        else:
            pbuf[d] = part
            ccopy(d).start()

    send_product(3)
    send_product(1)
    acopy(far, 0, True, 4).wait_recv()
    sibcopy(2, 0).start()
    acopy(far, 1, False, 5).wait_recv()
    sibcopy(2, 1).start()
    send_product(0)
    send_product(2)
    for d in (3, 1, 2):
        ccopy(d).wait_recv()
        pass_on(ypeer(NY - d))
    for d in range(1, NX):
        xcopy(xpeer(d), d).wait_recv()
    total = rsum[0].astype(F32) + rsum[1].astype(F32) + rsum[2].astype(F32) + rsum[3].astype(F32)
    out_ref[...] = total.astype(BF16)

    @pl.when(x != y)
    def _():
        for k in range(PIECES):
            flip(k).wait_send()

    for h in halos:
        h.wait_send()
    for n in range(PIECES * STEPS):
        for right in (True, False):
            if w_goes(n, right):
                wcopy(n, right).wait_send()
    for cp in to_mode + to_rows + to_back:
        cp.wait_send()
    for h in range(2):
        acopy(y, h, True, h).wait_send()
        acopy(y, h, False, 2 + h).wait_send()
    acopy(lhs, 0, True, 4).wait_send()
    acopy(rhs, 1, False, 5).wait_send()
    for d in range(NY):
        for h in range(2):
            sibcopy(d, h).wait_send()
    for d in range(1, NY):
        ccopy(d).wait_send()
    for d in range(1, NX):
        xcopy(xpeer(d), d).wait_send()


def local(
    query_rows, key_rows, value_rows, short_filter, decay_rate, residues, out_weight, record_starts
):
    vmem = pl.BlockSpec(memory_space=pltpu.VMEM)
    hbm = pl.BlockSpec(memory_space=pl.ANY)
    smem = pl.BlockSpec(memory_space=pltpu.SMEM)
    tokens = pltpu.VMEM((TOK * G, 128), F32)
    longer = pltpu.VMEM(((TOK + 2) * G, 128), F32)
    table = pltpu.VMEM((MODES * G, 128), F32)
    dma = pltpu.SemaphoreType.DMA
    return pl.pallas_call(
        kernel,
        out_shape=jax.ShapeDtypeStruct((TOK, COLS), BF16),
        in_specs=[hbm] * 7 + [smem],
        out_specs=vmem,
        scratch_shapes=[
            pltpu.VMEM((TOK, CH), BF16), pltpu.VMEM((TOK, CH), BF16), pltpu.VMEM((TOK, CH), BF16),
            pltpu.VMEM((3, KS, CH), F32), pltpu.VMEM((MODES, CH), F32), pltpu.VMEM((MODES, CH), F32),
            longer, longer, longer, tokens, tokens, tokens,
            pltpu.VMEM((9 * G, 128), F32), table, table, table, table,
            table, table, table, pltpu.VMEM((G, 128), F32), pltpu.VMEM((NY * G, 128), F32),
            pltpu.VMEM((G, 128), F32), table,
            pltpu.VMEM((NZ * TOK, COLS), BF16),
            pltpu.VMEM((NY, NC, TOK, CH), BF16),
            pltpu.VMEM((NY, TOK, COLS), BF16),
            pltpu.VMEM((NY, TOK, COLS), BF16),
            pltpu.VMEM((NX, TOK, COLS), BF16),
            dma((6,)), dma((3,)), dma((3,)), dma((2, PIECES)), dma((1,)), dma((2, 32)), dma((2, 32)),
            dma((NZ,)), dma((NZ,)), dma((NY,)), dma((NY,)), dma((NZ,)), dma((NZ,)),
            dma((6,)), dma((6,)), dma((NY, 2)), dma((NY, 2)),
            dma((NY,)), dma((NY,)), dma((NX,)), dma((NX,)),
        ],
        compiler_params=pltpu.CompilerParams(
            collective_id=0, has_side_effects=True, vmem_limit_bytes=60 * 1024 * 1024
        ),
    )(
        query_rows, key_rows, value_rows, short_filter,
        decay_rate.T, residues.T, out_weight, record_starts,
    )


def solution(mesh):
    return jax.shard_map(
        local,
        mesh=mesh,
        in_specs=(
            P("ctx", "ch"),
            P("ctx", "ch"),
            P("ctx", "ch"),
            P(None, None, "ch"),
            P("ch", None),
            P("ch", None),
            P("ctx", "ch"),
            P(),
        ),
        out_specs=P("ctx", "ch"),
        check_vma=False,
    )
```

```python
import functools

import jax
import jax.numpy as jnp
from jax import lax
from jax.experimental import pallas as pl
from jax.experimental.pallas import tpu as pltpu
from jax.sharding import PartitionSpec as P

MODES = 16
KS = 3
NX, NY, NZ, NC = 4, 4, 16, 2
TOK = 128
CH = 1024
G = CH // 128
COLS = 512
WIDE = COLS // 2
HALF = TOK // 2
PIECES = 4
PIECE = TOK // PIECES
MESH = pl.DeviceIdType.MESH
F32 = jnp.float32
BF16 = jnp.bfloat16


def exp_small(r):
    out = jnp.full_like(r, 1.0 / 5040.0)
    for c in (1.0 / 720.0, 1.0 / 120.0, 1.0 / 24.0, 1.0 / 6.0, 0.5, 1.0):
        out = c - r * out
    return 1.0 - r * out


def one_minus_exp(u):
    out = jnp.full_like(u, 1.0 / 40320.0)
    for c in (1.0 / 5040.0, 1.0 / 720.0, 1.0 / 120.0, 1.0 / 24.0, 1.0 / 6.0, 0.5, 1.0):
        out = c - u * out
    return u * out


def tree(parts):
    while len(parts) > 1:
        parts = [
            parts[i] + parts[i + 1] if i + 1 < len(parts) else parts[i]
            for i in range(0, len(parts), 2)
        ]
    return parts[0]


def kernel(
    q_in, k_in, v_in, sf_hbm, rate_hbm, res_hbm, w_in, rs,
    out_ref,
    q_raw, k_raw, v_raw, sf_in, rate_in, res_in, qt, kt, vt, xt, yt, gt, sft, ratet, rest, lamt, wt,
    fin, got, ebuf, rbuf, rgot, gref, ent, wbuf, abuf, pbuf, qbuf, rsum,
    load_sem, halo_send, halo_recv, tr_sem, keep_sem, wsend, wrecv,
    s1_send, s1_recv, s2_send, s2_recv, s3_send, s3_recv,
    a_send, a_recv, sib_send, sib_recv, c_send, c_recv, x_send, x_recv,
):
    ctx = lax.axis_index("ctx")
    ch = lax.axis_index("ch")
    y, z = ctx // NZ, lax.rem(ctx, NZ)
    x, c = ch // NC, lax.rem(ch, NC)

    def dev(xx, cc, yy, zz):
        return (yy * NZ + zz, xx * NC + cc)

    def zpeer(d):
        return lax.rem(z + d, NZ)

    def ypeer(d):
        return lax.rem(y + d, NY)

    def xpeer(d):
        return lax.rem(x + d, NX)

    n_ctx = NY * NZ
    after = (lax.rem(ctx + 1, n_ctx), ch)
    before = (lax.rem(ctx + n_ctx - 1, n_ctx), ch)
    sibling = dev(x, 1 - c, y, z)
    flipped = dev(y, c, x, z)

    loads = [
        pltpu.make_async_copy(src, dst, load_sem.at[i])
        for i, (src, dst) in enumerate(
            (
                (k_in, k_raw), (v_in, v_raw), (q_in, q_raw),
                (rate_hbm, rate_in), (res_hbm, res_in), (sf_hbm, sf_in),
            )
        )
    ]
    for load in loads:
        load.start()

    barrier = pltpu.get_barrier_semaphore()

    def greet(d):
        pl.semaphore_signal(barrier, inc=1, device_id=d, device_id_type=MESH)

    for d in range(1, NZ):
        greet(dev(x, c, y, zpeer(d)))
    for d in range(1, NY):
        greet(dev(x, c, ypeer(d), z))
    for d in range(1, NX):
        greet(dev(xpeer(d), c, y, z))
    greet(sibling)
    greet(before)
    greet(after)

    @pl.when(x != y)
    def _():
        greet(flipped)

    partners = (NZ - 1) + (NY - 1) + (NX - 1) + 3 + jnp.where(x != y, 1, 0)
    pl.semaphore_wait(barrier, partners)

    halos = []
    for i, arr in enumerate((kt, vt, qt)):
        halos.append(
            pltpu.make_async_remote_copy(
                src_ref=arr.at[pl.ds(TOK * G, 2 * G), :],
                dst_ref=arr.at[pl.ds(0, 2 * G), :],
                send_sem=halo_send.at[i],
                recv_sem=halo_recv.at[i],
                device_id=after,
                device_id_type=MESH,
            )
        )

    def wslot(s):
        return wbuf.at[pl.ds(pl.multiple_of(s * TOK, TOK), TOK), :]

    def wpart(s, first, count):
        return wbuf.at[pl.ds(pl.multiple_of(s * TOK + first, PIECE), count), :]

    def flip(k):
        return pltpu.make_async_remote_copy(
            src_ref=w_in.at[pl.ds(k * PIECE, PIECE), :],
            dst_ref=wpart(z, k * PIECE, PIECE),
            send_sem=tr_sem.at[0, k],
            recv_sem=tr_sem.at[1, k],
            device_id=flipped,
            device_id_type=MESH,
        )

    keep_w = pltpu.make_async_copy(w_in, wslot(z), keep_sem.at[0])

    @pl.when(x != y)
    def _():
        for k in range(PIECES):
            flip(k).start()

    @pl.when(x == y)
    def _():
        keep_w.start()

    def spread(raw, dst, first, count):
        for g in range(G):
            lanes = slice(g * 128, (g + 1) * 128)
            dst[pl.ds((2 + first) * G + g, count, stride=G), :] = raw[first : first + count, lanes].astype(F32)

    for i, (raw, dst) in enumerate(((k_raw, kt), (v_raw, vt))):
        loads[i].wait()
        spread(raw, dst, TOK - 16, 16)
        halos[i].start()

    for load in loads[3:]:
        load.wait()
    for g in range(G):
        lanes = slice(g * 128, (g + 1) * 128)
        ratet[pl.ds(g, MODES, stride=G), :] = rate_in[:, lanes]
        rest[pl.ds(g, MODES, stride=G), :] = res_in[:, lanes]
        for i in range(3):
            sft[pl.ds(i * KS * G + g, KS, stride=G), :] = sf_in[i, :, lanes]
    rate_all = ratet[...]
    lamt[...] = exp_small(rate_all)
    wt[...] = rest[...] * jnp.sqrt(one_minus_exp(2.0 * rate_all))

    spread(k_raw, kt, 0, TOK - 16)
    spread(v_raw, vt, 0, TOK - 16)
    loads[2].wait()
    spread(q_raw, qt, TOK - 16, 16)
    halos[2].start()
    spread(q_raw, qt, 0, TOK - 16)

    STEPS = NZ // 2

    def wcopy(n, right):
        hop, part = n // PIECES, n % PIECES
        slot = lax.rem(z + NZ - hop, NZ) if right else lax.rem(z + hop, NZ)
        side = 0 if right else 1
        return pltpu.make_async_remote_copy(
            src_ref=wpart(slot, part * PIECE, PIECE),
            dst_ref=wpart(slot, part * PIECE, PIECE),
            send_sem=wsend.at[side, n],
            recv_sem=wrecv.at[side, n],
            device_id=dev(x, c, y, zpeer(1 if right else NZ - 1)),
            device_id_type=MESH,
        )

    def w_goes(n, right):
        return n < PIECES * STEPS and (n // PIECES < STEPS - 1 or (n % 2 == 0) == right)

    def w_step(n):
        if n < PIECES:
            @pl.when(x != y)
            def _():
                flip(n).wait_recv()

            if n == 0:
                @pl.when(x == y)
                def _():
                    keep_w.wait()

        for right in (True, False):
            if n >= PIECES and w_goes(n - PIECES, right):
                wcopy(n - PIECES, right).wait_recv()
            if w_goes(n, right):
                wcopy(n, right).start()

    def w_hop(h):
        for part in range(PIECES):
            w_step(h * PIECES + part)

    base = ctx * TOK
    starts = [rs[i] for i in range(4)]

    def seg_of(pos):
        seg = jnp.int32(0)
        for st in starts:
            seg = jnp.maximum(seg, jnp.where(st <= pos, st, 0))
        return seg

    def tile(ref, t):
        return ref[pl.ds(pl.multiple_of(t * G, G), G), :]

    def put(ref, t, val):
        ref[pl.ds(pl.multiple_of(t * G, G), G), :] = val

    def age_masks(pos):
        age = pos - seg_of(pos)
        return jnp.where(age >= 1, 1.0, 0.0).astype(F32), jnp.where(age >= 2, 1.0, 0.0).astype(F32)

    def taps(i):
        return [sft[(i * KS + j) * G : (i * KS + j + 1) * G, :] for j in range(KS)]

    def conv(ref, w, t, m1, m2):
        return w[0] * tile(ref, t + 2) + w[1] * tile(ref, t + 1) * m1 + w[2] * tile(ref, t) * m2

    def mix(t):
        m1, m2 = age_masks(base + t)
        return (conv(kt, taps(1), t, m1, m2) * conv(vt, taps(2), t, m1, m2)).astype(BF16).astype(F32)

    lams = lambda: [lamt[m * G : (m + 1) * G, :] for m in range(MODES)]
    ws = lambda: [wt[m * G : (m + 1) * G, :] for m in range(MODES)]
    last_seg = seg_of(base + TOK - 1)

    def pass1(i, state):
        lam = lams()
        for u in range(6):
            t = 2 + i * 6 + u
            val = mix(t)
            put(xt, t, val)
            val = val * jnp.where(base + t >= last_seg, 1.0, 0.0).astype(F32)
            state = [s * l + val for s, l in zip(state, lam)]
        return state

    zero = jnp.zeros((G, 128), F32)
    state = lax.fori_loop(0, (TOK - 2) // 6, pass1, [zero] * MODES)
    halos[0].wait_recv()
    halos[1].wait_recv()
    val0, val1 = mix(0), mix(1)
    put(xt, 0, val0)
    put(xt, 1, val1)
    val0 = val0 * jnp.where(base >= last_seg, 1.0, 0.0).astype(F32)
    val1 = val1 * jnp.where(base + 1 >= last_seg, 1.0, 0.0).astype(F32)
    for m in range(MODES):
        rows = slice(m * G, (m + 1) * G)
        far = jnp.exp(ratet[rows, :] * (-(TOK - 2.0)))
        fin[rows, :] = state[m] + far * (lamt[rows, :] * val0 + val1)

    def zexchange(src, dst, send, recv):
        def one(d):
            peer = zpeer(d)
            return pltpu.make_async_remote_copy(
                src_ref=src.at[pl.ds(pl.multiple_of(peer * G, G), G), :],
                dst_ref=dst.at[pl.ds(pl.multiple_of(z * G, G), G), :],
                send_sem=send.at[d],
                recv_sem=recv.at[d],
                device_id=dev(x, c, y, peer),
                device_id_type=MESH,
            )

        return [one(d) for d in range(1, NZ)]

    to_mode = zexchange(fin, got, s1_send, s1_recv)
    for cp in to_mode:
        cp.start()
    put(got, z, tile(fin, z))

    halos[2].wait_recv()

    def qconv(i, carry):
        for u in range(8):
            t = i * 8 + u
            m1, m2 = age_masks(base + t)
            put(gt, t, conv(qt, taps(0), t, m1, m2))
        return carry

    def local_part(i, state):
        lam, w = lams(), ws()
        for u in range(8):
            t = i * 8 + u
            val = tile(xt, t)
            m1, _ = age_masks(base + t)
            state = [s * m1 * l + val for s, l in zip(state, lam)]
            put(yt, t, tree([a * b for a, b in zip(w, state)]))
        return state

    lax.fori_loop(0, TOK // 8, qconv, 0)
    state = lax.fori_loop(0, TOK // 16, local_part, [zero] * MODES)
    w_hop(0)
    state = lax.fori_loop(TOK // 16, TOK // 8, local_part, state)
    w_hop(1)

    def unbroken(first, count):
        hit = jnp.int32(0)
        for st in starts:
            hit = hit + jnp.where((st >= first) & (st < first + count), 1, 0)
        return jnp.where(hit == 0, 1.0, 0.0).astype(F32)

    for cp in to_mode:
        cp.wait_recv()
    rate_m = tile(ratet, z)
    one_block = jnp.exp(rate_m * (-float(TOK)))
    one_row = jnp.exp(rate_m * (-float(TOK * NZ)))
    entry = zero
    for zz in range(NZ):
        ebuf[zz * G : (zz + 1) * G, :] = entry
        entry = entry * (one_block * unbroken((y * NZ + zz) * TOK, TOK)) + got[zz * G : (zz + 1) * G, :]
    rbuf[...] = entry

    to_rows = [
        pltpu.make_async_remote_copy(
            src_ref=rbuf,
            dst_ref=rgot.at[pl.ds(pl.multiple_of(y * G, G), G), :],
            send_sem=s2_send.at[d],
            recv_sem=s2_recv.at[d],
            device_id=dev(x, c, ypeer(d), z),
            device_id_type=MESH,
        )
        for d in range(1, NY)
    ]
    for cp in to_rows:
        cp.start()
    w_hop(2)
    for cp in to_rows:
        cp.wait_recv()
    gref[...] = zero
    for yy in range(NY - 1):
        @pl.when(yy < y)
        def _():
            gref[...] = gref[...] * (one_row * unbroken(yy * NZ * TOK, NZ * TOK)) + rgot[yy * G : (yy + 1) * G, :]

    entry = gref[...]
    for zz in range(NZ):
        rows = slice(zz * G, (zz + 1) * G)
        ebuf[rows, :] = ebuf[rows, :] + entry
        entry = entry * (one_block * unbroken((y * NZ + zz) * TOK, TOK))
    to_back = zexchange(ebuf, ent, s3_send, s3_recv)
    for cp in to_back:
        cp.start()
    put(ent, z, tile(ebuf, z))
    for hop in (3, 4):
        w_hop(hop)
    for cp in to_back:
        cp.wait_recv()

    def correct(i, state):
        lam = lams()
        for u in range(8):
            t = i * 8 + u
            free = jnp.where(seg_of(base + t) < base, 1.0, 0.0).astype(F32)
            filtered = tile(yt, t) + tree(list(state)) * free
            put(gt, t, tile(gt, t) * filtered)
            state = [s * l for s, l in zip(state, lam)]
        return state

    init = []
    for m in range(MODES):
        rows = slice(m * G, (m + 1) * G)
        init.append(ent[rows, :] * lamt[rows, :] * wt[rows, :])
    state = init

    def ablock(yy, cc, h):
        return abuf.at[cc, pl.ds(pl.multiple_of(yy * TOK + h * HALF, HALF), HALF), :]

    def acopy(yy, h, right, index):
        return pltpu.make_async_remote_copy(
            src_ref=ablock(yy, c, h),
            dst_ref=ablock(yy, c, h),
            send_sem=a_send.at[index],
            recv_sem=a_recv.at[index],
            device_id=dev(x, c, ypeer(1 if right else NY - 1), z),
            device_id_type=MESH,
        )

    def sibcopy(d, h):
        yy = ypeer(d)
        return pltpu.make_async_remote_copy(
            src_ref=ablock(yy, c, h),
            dst_ref=ablock(yy, c, h),
            send_sem=sib_send.at[d, h],
            recv_sem=sib_recv.at[d, h],
            device_id=sibling,
            device_id_type=MESH,
        )

    for h in range(2):
        state = lax.fori_loop(h * (TOK // 16), (h + 1) * (TOK // 16), correct, state)
        for g in range(G):
            part = gt[pl.ds(h * HALF * G + g, HALF, stride=G), :].astype(BF16)
            abuf[c, pl.ds(pl.multiple_of(y * TOK + h * HALF, HALF), HALF), g * 128 : (g + 1) * 128] = part
        if h == 1:
            acopy(y, 1, False, 3).start()
        acopy(y, h, True, h).start()
        sibcopy(0, h).start()
        if h == 0:
            w_hop(5)
    acopy(y, 0, False, 2).start()

    lhs, rhs, far = ypeer(NY - 1), ypeer(1), ypeer(2)
    w_hop(6)
    acopy(y, 0, True, 0).wait_recv()
    acopy(lhs, 0, True, 4).start()
    sibcopy(3, 0).start()
    acopy(y, 1, False, 3).wait_recv()
    acopy(rhs, 1, False, 5).start()
    sibcopy(1, 1).start()
    w_hop(7)
    acopy(y, 1, True, 1).wait_recv()
    sibcopy(3, 1).start()
    acopy(y, 0, False, 2).wait_recv()
    sibcopy(1, 0).start()
    w_hop(8)
    def product(d, k):
        rows = pl.ds(pl.multiple_of(ypeer(d) * TOK, TOK), TOK)
        cols = slice(k * WIDE, (k + 1) * WIDE)
        acc = jnp.dot(abuf[0, rows, :], wbuf[0:CH, cols], preferred_element_type=F32)
        acc = acc + jnp.dot(abuf[1, rows, :], wbuf[CH : 2 * CH, cols], preferred_element_type=F32)
        pbuf[k, rows, :] = acc.astype(BF16)

    def ccopy(d, k):
        return pltpu.make_async_remote_copy(
            src_ref=pbuf.at[k, pl.ds(pl.multiple_of(ypeer(d) * TOK, TOK), TOK), :],
            dst_ref=qbuf.at[y, k],
            send_sem=c_send.at[d, k],
            recv_sem=c_recv.at[d, k],
            device_id=dev(x, c, ypeer(d), z),
            device_id_type=MESH,
        )

    for d in (1, 3):
        for h in range(2):
            sibcopy(d, h).wait_recv()
        for k in range(2):
            product(d, k)
            ccopy(d, k).start()
    acopy(far, 0, True, 4).wait_recv()
    sibcopy(2, 0).start()
    acopy(far, 1, False, 5).wait_recv()
    sibcopy(2, 1).start()

    def xcopy(o, d, k):
        return pltpu.make_async_remote_copy(
            src_ref=qbuf.at[o, k],
            dst_ref=rsum.at[x, k],
            send_sem=x_send.at[d, k],
            recv_sem=x_recv.at[d, k],
            device_id=dev(o, c, y, z),
            device_id_type=MESH,
        )

    def pass_on(o, k):
        for d in range(1, NX):
            @pl.when(o == xpeer(d))
            def _():
                xcopy(xpeer(d), d, k).start()

        @pl.when(o == x)
        def _():
            rsum[x, k] = qbuf[o, k]

    for d in (0, 2):
        for h in range(2):
            sibcopy(d, h).wait_recv()
    for k in range(2):
        product(2, k)
        ccopy(2, k).start()
    for k in range(2):
        product(0, k)
        qbuf[y, k] = pbuf[k, pl.ds(pl.multiple_of(y * TOK, TOK), TOK), :]
        pass_on(y, k)
    @pl.when(x != y)
    def _():
        for k in range(PIECES):
            flip(k).wait_send()

    for h in halos:
        h.wait_send()
    for n in range(PIECES * STEPS):
        for right in (True, False):
            if w_goes(n, right):
                wcopy(n, right).wait_send()
    for cp in to_mode + to_rows + to_back:
        cp.wait_send()
    for h in range(2):
        acopy(y, h, True, h).wait_send()
        acopy(y, h, False, 2 + h).wait_send()
    acopy(lhs, 0, True, 4).wait_send()
    acopy(rhs, 1, False, 5).wait_send()
    for d in range(NY):
        for h in range(2):
            sibcopy(d, h).wait_send()

    for k in range(2):
        for d in (3, 1, 2):
            ccopy(d, k).wait_recv()
            pass_on(ypeer(NY - d), k)
    for k in range(2):
        for d in range(1, NX):
            xcopy(xpeer(d), d, k).wait_recv()
        total = tree([rsum[i, k].astype(F32) for i in range(NX)])
        out_ref[:, k * WIDE : (k + 1) * WIDE] = total.astype(BF16)

    for d in range(1, NY):
        for k in range(2):
            ccopy(d, k).wait_send()
    for d in range(1, NX):
        for k in range(2):
            xcopy(xpeer(d), d, k).wait_send()


def local(
    query_rows, key_rows, value_rows, short_filter, decay_rate, residues, out_weight, record_starts
):
    vmem = pl.BlockSpec(memory_space=pltpu.VMEM)
    hbm = pl.BlockSpec(memory_space=pl.ANY)
    smem = pl.BlockSpec(memory_space=pltpu.SMEM)
    tokens = pltpu.VMEM((TOK * G, 128), F32)
    longer = pltpu.VMEM(((TOK + 2) * G, 128), F32)
    table = pltpu.VMEM((MODES * G, 128), F32)
    dma = pltpu.SemaphoreType.DMA
    return pl.pallas_call(
        kernel,
        out_shape=jax.ShapeDtypeStruct((TOK, COLS), BF16),
        in_specs=[hbm] * 7 + [smem],
        out_specs=vmem,
        scratch_shapes=[
            pltpu.VMEM((TOK, CH), BF16), pltpu.VMEM((TOK, CH), BF16), pltpu.VMEM((TOK, CH), BF16),
            pltpu.VMEM((3, KS, CH), F32), pltpu.VMEM((MODES, CH), F32), pltpu.VMEM((MODES, CH), F32),
            longer, longer, longer, tokens, tokens, tokens,
            pltpu.VMEM((9 * G, 128), F32), table, table, table, table,
            table, table, table, pltpu.VMEM((G, 128), F32), pltpu.VMEM((NY * G, 128), F32),
            pltpu.VMEM((G, 128), F32), table,
            pltpu.VMEM((NZ * TOK, COLS), BF16),
            pltpu.VMEM((NC, NY * TOK, CH), BF16),
            pltpu.VMEM((2, NY * TOK, WIDE), BF16),
            pltpu.VMEM((NY, 2, TOK, WIDE), BF16),
            pltpu.VMEM((NX, 2, TOK, WIDE), BF16),
            dma((6,)), dma((3,)), dma((3,)), dma((2, PIECES)), dma((1,)), dma((2, 32)), dma((2, 32)),
            dma((NZ,)), dma((NZ,)), dma((NY,)), dma((NY,)), dma((NZ,)), dma((NZ,)),
            dma((6,)), dma((6,)), dma((NY, 2)), dma((NY, 2)),
            dma((NY, 2)), dma((NY, 2)), dma((NX, 2)), dma((NX, 2)),
        ],
        compiler_params=pltpu.CompilerParams(
            collective_id=0, has_side_effects=True, vmem_limit_bytes=60 * 1024 * 1024
        ),
    )(
        query_rows, key_rows, value_rows, short_filter,
        decay_rate.T, residues.T, out_weight, record_starts,
    )


def solution(mesh):
    return jax.shard_map(
        local,
        mesh=mesh,
        in_specs=(
            P("ctx", "ch"),
            P("ctx", "ch"),
            P("ctx", "ch"),
            P(None, None, "ch"),
            P("ch", None),
            P("ch", None),
            P("ctx", "ch"),
            P(),
        ),
        out_specs=P("ctx", "ch"),
        check_vma=False,
    )
```

```python
import functools

import jax
import jax.numpy as jnp
from jax import lax
from jax.experimental import pallas as pl
from jax.experimental.pallas import tpu as pltpu
from jax.sharding import PartitionSpec as P

MODES = 16
KS = 3
NX, NY, NZ, NC = 4, 4, 16, 2
TOK = 128
CH = 1024
G = CH // 128
COLS = 512
WIDE = COLS // 2
HALF = TOK // 2
PIECES = 4
PIECE = TOK // PIECES
MESH = pl.DeviceIdType.MESH
F32 = jnp.float32
BF16 = jnp.bfloat16


def exp_small(r):
    out = jnp.full_like(r, 1.0 / 5040.0)
    for c in (1.0 / 720.0, 1.0 / 120.0, 1.0 / 24.0, 1.0 / 6.0, 0.5, 1.0):
        out = c - r * out
    return 1.0 - r * out


def one_minus_exp(u):
    out = jnp.full_like(u, 1.0 / 40320.0)
    for c in (1.0 / 5040.0, 1.0 / 720.0, 1.0 / 120.0, 1.0 / 24.0, 1.0 / 6.0, 0.5, 1.0):
        out = c - u * out
    return u * out


def tree(parts):
    while len(parts) > 1:
        parts = [
            parts[i] + parts[i + 1] if i + 1 < len(parts) else parts[i]
            for i in range(0, len(parts), 2)
        ]
    return parts[0]


def kernel(
    q_in, k_in, v_in, sf_hbm, rate_hbm, res_hbm, w_in, rs,
    out_ref,
    q_raw, k_raw, v_raw, sf_in, rate_in, res_in, qt, kt, vt, xt, yt, gt, sft, ratet, rest, lamt, wt,
    fin, got, ebuf, rbuf, rgot, gref, ent, wbuf, abuf, pbuf, qbuf, rsum,
    load_sem, halo_send, halo_recv, tr_sem, keep_sem, wsend, wrecv,
    s1_send, s1_recv, s2_send, s2_recv, s3_send, s3_recv,
    a_send, a_recv, sib_send, sib_recv, c_send, c_recv, x_send, x_recv,
):
    ctx = lax.axis_index("ctx")
    ch = lax.axis_index("ch")
    y, z = ctx // NZ, lax.rem(ctx, NZ)
    x, c = ch // NC, lax.rem(ch, NC)

    def dev(xx, cc, yy, zz):
        return (yy * NZ + zz, xx * NC + cc)

    def zpeer(d):
        return lax.rem(z + d, NZ)

    def ypeer(d):
        return lax.rem(y + d, NY)

    def xpeer(d):
        return lax.rem(x + d, NX)

    n_ctx = NY * NZ
    after = (lax.rem(ctx + 1, n_ctx), ch)
    before = (lax.rem(ctx + n_ctx - 1, n_ctx), ch)
    sibling = dev(x, 1 - c, y, z)
    flipped = dev(y, c, x, z)

    loads = [
        pltpu.make_async_copy(src, dst, load_sem.at[i])
        for i, (src, dst) in enumerate(
            (
                (k_in, k_raw), (v_in, v_raw), (q_in, q_raw),
                (rate_hbm, rate_in), (res_hbm, res_in), (sf_hbm, sf_in),
            )
        )
    ]
    for load in loads:
        load.start()

    barrier = pltpu.get_barrier_semaphore()

    def greet(d):
        pl.semaphore_signal(barrier, inc=1, device_id=d, device_id_type=MESH)

    for d in range(1, NZ):
        greet(dev(x, c, y, zpeer(d)))
    for d in range(1, NY):
        greet(dev(x, c, ypeer(d), z))
    for d in range(1, NX):
        greet(dev(xpeer(d), c, y, z))
    greet(sibling)
    greet(before)
    greet(after)

    @pl.when(x != y)
    def _():
        greet(flipped)

    partners = (NZ - 1) + (NY - 1) + (NX - 1) + 3 + jnp.where(x != y, 1, 0)
    pl.semaphore_wait(barrier, partners)

    halos = []
    for i, arr in enumerate((kt, vt, qt)):
        halos.append(
            pltpu.make_async_remote_copy(
                src_ref=arr.at[pl.ds(TOK * G, 2 * G), :],
                dst_ref=arr.at[pl.ds(0, 2 * G), :],
                send_sem=halo_send.at[i],
                recv_sem=halo_recv.at[i],
                device_id=after,
                device_id_type=MESH,
            )
        )

    def wslot(s):
        return wbuf.at[pl.ds(pl.multiple_of(s * TOK, TOK), TOK), :]

    def wpart(s, first, count):
        return wbuf.at[pl.ds(pl.multiple_of(s * TOK + first, PIECE), count), :]

    def flip(k):
        return pltpu.make_async_remote_copy(
            src_ref=w_in.at[pl.ds(k * PIECE, PIECE), :],
            dst_ref=wpart(z, k * PIECE, PIECE),
            send_sem=tr_sem.at[0, k],
            recv_sem=tr_sem.at[1, k],
            device_id=flipped,
            device_id_type=MESH,
        )

    keep_w = pltpu.make_async_copy(w_in, wslot(z), keep_sem.at[0])

    @pl.when(x != y)
    def _():
        for k in range(PIECES):
            flip(k).start()

    @pl.when(x == y)
    def _():
        keep_w.start()

    def spread(raw, dst, first, count):
        for g in range(G):
            lanes = slice(g * 128, (g + 1) * 128)
            dst[pl.ds((2 + first) * G + g, count, stride=G), :] = raw[first : first + count, lanes].astype(F32)

    for i, (raw, dst) in enumerate(((k_raw, kt), (v_raw, vt))):
        loads[i].wait()
        spread(raw, dst, TOK - 16, 16)
        halos[i].start()

    for load in loads[3:]:
        load.wait()
    for g in range(G):
        lanes = slice(g * 128, (g + 1) * 128)
        ratet[pl.ds(g, MODES, stride=G), :] = rate_in[:, lanes]
        rest[pl.ds(g, MODES, stride=G), :] = res_in[:, lanes]
        for i in range(3):
            sft[pl.ds(i * KS * G + g, KS, stride=G), :] = sf_in[i, :, lanes]
    rate_all = ratet[...]
    lamt[...] = exp_small(rate_all)
    wt[...] = rest[...] * jnp.sqrt(one_minus_exp(2.0 * rate_all))

    spread(k_raw, kt, 0, TOK - 16)
    spread(v_raw, vt, 0, TOK - 16)
    loads[2].wait()
    spread(q_raw, qt, TOK - 16, 16)
    halos[2].start()
    spread(q_raw, qt, 0, TOK - 16)

    STEPS = NZ // 2

    def wcopy(n, right):
        hop, part = n // PIECES, n % PIECES
        slot = lax.rem(z + NZ - hop, NZ) if right else lax.rem(z + hop, NZ)
        side = 0 if right else 1
        return pltpu.make_async_remote_copy(
            src_ref=wpart(slot, part * PIECE, PIECE),
            dst_ref=wpart(slot, part * PIECE, PIECE),
            send_sem=wsend.at[side, n],
            recv_sem=wrecv.at[side, n],
            device_id=dev(x, c, y, zpeer(1 if right else NZ - 1)),
            device_id_type=MESH,
        )

    def w_goes(n, right):
        return n < PIECES * STEPS and (n // PIECES < STEPS - 1 or (n % 2 == 0) == right)

    def w_step(n):
        if n < PIECES:
            @pl.when(x != y)
            def _():
                flip(n).wait_recv()

            if n == 0:
                @pl.when(x == y)
                def _():
                    keep_w.wait()

        for right in (True, False):
            if n >= PIECES and w_goes(n - PIECES, right):
                wcopy(n - PIECES, right).wait_recv()
            if w_goes(n, right):
                wcopy(n, right).start()

    def w_hop(h):
        for part in range(PIECES):
            w_step(h * PIECES + part)

    base = ctx * TOK
    starts = [rs[i] for i in range(4)]

    def seg_of(pos):
        seg = jnp.int32(0)
        for st in starts:
            seg = jnp.maximum(seg, jnp.where(st <= pos, st, 0))
        return seg

    def tile(ref, t):
        return ref[pl.ds(pl.multiple_of(t * G, G), G), :]

    def put(ref, t, val):
        ref[pl.ds(pl.multiple_of(t * G, G), G), :] = val

    def age_masks(pos):
        age = pos - seg_of(pos)
        return jnp.where(age >= 1, 1.0, 0.0).astype(F32), jnp.where(age >= 2, 1.0, 0.0).astype(F32)

    def taps(i):
        return [sft[(i * KS + j) * G : (i * KS + j + 1) * G, :] for j in range(KS)]

    def conv(ref, w, t, m1, m2):
        return w[0] * tile(ref, t + 2) + w[1] * tile(ref, t + 1) * m1 + w[2] * tile(ref, t) * m2

    def mix(t):
        m1, m2 = age_masks(base + t)
        return (conv(kt, taps(1), t, m1, m2) * conv(vt, taps(2), t, m1, m2)).astype(BF16).astype(F32)

    lams = lambda: [lamt[m * G : (m + 1) * G, :] for m in range(MODES)]
    ws = lambda: [wt[m * G : (m + 1) * G, :] for m in range(MODES)]
    last_seg = seg_of(base + TOK - 1)

    def pass1(i, state):
        lam = lams()
        for u in range(6):
            t = 2 + i * 6 + u
            val = mix(t)
            put(xt, t, val)
            val = val * jnp.where(base + t >= last_seg, 1.0, 0.0).astype(F32)
            state = [s * l + val for s, l in zip(state, lam)]
        return state

    zero = jnp.zeros((G, 128), F32)
    state = lax.fori_loop(0, (TOK - 2) // 6, pass1, [zero] * MODES)
    halos[0].wait_recv()
    halos[1].wait_recv()
    val0, val1 = mix(0), mix(1)
    put(xt, 0, val0)
    put(xt, 1, val1)
    val0 = val0 * jnp.where(base >= last_seg, 1.0, 0.0).astype(F32)
    val1 = val1 * jnp.where(base + 1 >= last_seg, 1.0, 0.0).astype(F32)
    for m in range(MODES):
        rows = slice(m * G, (m + 1) * G)
        far = jnp.exp(ratet[rows, :] * (-(TOK - 2.0)))
        fin[rows, :] = state[m] + far * (lamt[rows, :] * val0 + val1)

    def zexchange(src, dst, send, recv):
        def one(d):
            peer = zpeer(d)
            return pltpu.make_async_remote_copy(
                src_ref=src.at[pl.ds(pl.multiple_of(peer * G, G), G), :],
                dst_ref=dst.at[pl.ds(pl.multiple_of(z * G, G), G), :],
                send_sem=send.at[d],
                recv_sem=recv.at[d],
                device_id=dev(x, c, y, peer),
                device_id_type=MESH,
            )

        return [one(d) for d in range(1, NZ)]

    to_mode = zexchange(fin, got, s1_send, s1_recv)
    for cp in to_mode:
        cp.start()
    put(got, z, tile(fin, z))

    halos[2].wait_recv()

    def qconv(i, carry):
        for u in range(8):
            t = i * 8 + u
            m1, m2 = age_masks(base + t)
            put(gt, t, conv(qt, taps(0), t, m1, m2))
        return carry

    def local_part(i, state):
        lam, w = lams(), ws()
        for u in range(8):
            t = i * 8 + u
            val = tile(xt, t)
            m1, _ = age_masks(base + t)
            state = [s * m1 * l + val for s, l in zip(state, lam)]
            put(yt, t, tree([a * b for a, b in zip(w, state)]))
        return state

    lax.fori_loop(0, TOK // 8, qconv, 0)
    state = lax.fori_loop(0, TOK // 16, local_part, [zero] * MODES)
    w_hop(0)
    state = lax.fori_loop(TOK // 16, TOK // 8, local_part, state)
    w_hop(1)

    def unbroken(first, count):
        hit = jnp.int32(0)
        for st in starts:
            hit = hit + jnp.where((st >= first) & (st < first + count), 1, 0)
        return jnp.where(hit == 0, 1.0, 0.0).astype(F32)

    for cp in to_mode:
        cp.wait_recv()
    rate_m = tile(ratet, z)
    one_block = jnp.exp(rate_m * (-float(TOK)))
    one_row = jnp.exp(rate_m * (-float(TOK * NZ)))
    entry = zero
    for zz in range(NZ):
        ebuf[zz * G : (zz + 1) * G, :] = entry
        entry = entry * (one_block * unbroken((y * NZ + zz) * TOK, TOK)) + got[zz * G : (zz + 1) * G, :]
    rbuf[...] = entry

    to_rows = [
        pltpu.make_async_remote_copy(
            src_ref=rbuf,
            dst_ref=rgot.at[pl.ds(pl.multiple_of(y * G, G), G), :],
            send_sem=s2_send.at[d],
            recv_sem=s2_recv.at[d],
            device_id=dev(x, c, ypeer(d), z),
            device_id_type=MESH,
        )
        for d in range(1, NY)
    ]
    for cp in to_rows:
        cp.start()
    w_hop(2)
    for cp in to_rows:
        cp.wait_recv()
    gref[...] = zero
    for yy in range(NY - 1):
        @pl.when(yy < y)
        def _():
            gref[...] = gref[...] * (one_row * unbroken(yy * NZ * TOK, NZ * TOK)) + rgot[yy * G : (yy + 1) * G, :]

    entry = gref[...]
    for zz in range(NZ):
        rows = slice(zz * G, (zz + 1) * G)
        ebuf[rows, :] = ebuf[rows, :] + entry
        entry = entry * (one_block * unbroken((y * NZ + zz) * TOK, TOK))
    to_back = zexchange(ebuf, ent, s3_send, s3_recv)
    for cp in to_back:
        cp.start()
    put(ent, z, tile(ebuf, z))
    for hop in (3, 4):
        w_hop(hop)
    for cp in to_back:
        cp.wait_recv()

    def correct(i, state):
        lam = lams()
        for u in range(8):
            t = i * 8 + u
            free = jnp.where(seg_of(base + t) < base, 1.0, 0.0).astype(F32)
            filtered = tile(yt, t) + tree(list(state)) * free
            put(gt, t, tile(gt, t) * filtered)
            state = [s * l for s, l in zip(state, lam)]
        return state

    init = []
    for m in range(MODES):
        rows = slice(m * G, (m + 1) * G)
        init.append(ent[rows, :] * lamt[rows, :] * wt[rows, :])
    state = init

    def ablock(yy, cc, h):
        return abuf.at[cc, pl.ds(pl.multiple_of(yy * TOK + h * HALF, HALF), HALF), :]

    def acopy(yy, h, right, index):
        return pltpu.make_async_remote_copy(
            src_ref=ablock(yy, c, h),
            dst_ref=ablock(yy, c, h),
            send_sem=a_send.at[index],
            recv_sem=a_recv.at[index],
            device_id=dev(x, c, ypeer(1 if right else NY - 1), z),
            device_id_type=MESH,
        )

    def sibcopy(d, h):
        yy = ypeer(d)
        return pltpu.make_async_remote_copy(
            src_ref=ablock(yy, c, h),
            dst_ref=ablock(yy, c, h),
            send_sem=sib_send.at[d, h],
            recv_sem=sib_recv.at[d, h],
            device_id=sibling,
            device_id_type=MESH,
        )

    for h in range(2):
        state = lax.fori_loop(h * (TOK // 16), (h + 1) * (TOK // 16), correct, state)
        for g in range(G):
            part = gt[pl.ds(h * HALF * G + g, HALF, stride=G), :].astype(BF16)
            abuf[c, pl.ds(pl.multiple_of(y * TOK + h * HALF, HALF), HALF), g * 128 : (g + 1) * 128] = part
        if h == 1:
            acopy(y, 1, False, 3).start()
        acopy(y, h, True, h).start()
        sibcopy(0, h).start()
        if h == 0:
            w_hop(5)
    acopy(y, 0, False, 2).start()

    lhs, rhs, far = ypeer(NY - 1), ypeer(1), ypeer(2)
    w_hop(6)
    acopy(y, 0, True, 0).wait_recv()
    acopy(lhs, 0, True, 4).start()
    sibcopy(3, 0).start()
    acopy(y, 1, False, 3).wait_recv()
    acopy(rhs, 1, False, 5).start()
    sibcopy(1, 1).start()
    w_hop(7)
    acopy(y, 1, True, 1).wait_recv()
    sibcopy(3, 1).start()
    acopy(y, 0, False, 2).wait_recv()
    sibcopy(1, 0).start()
    w_hop(8)
    def product(d, k):
        rows = pl.ds(pl.multiple_of(ypeer(d) * TOK, TOK), TOK)
        cols = slice(k * WIDE, (k + 1) * WIDE)
        acc = jnp.dot(abuf[0, rows, :], wbuf[0:CH, cols], preferred_element_type=F32)
        acc = acc + jnp.dot(abuf[1, rows, :], wbuf[CH : 2 * CH, cols], preferred_element_type=F32)
        pbuf[k, rows, :] = acc.astype(BF16)

    def ccopy(d, k):
        return pltpu.make_async_remote_copy(
            src_ref=pbuf.at[k, pl.ds(pl.multiple_of(ypeer(d) * TOK, TOK), TOK), :],
            dst_ref=qbuf.at[y, k],
            send_sem=c_send.at[d, k],
            recv_sem=c_recv.at[d, k],
            device_id=dev(x, c, ypeer(d), z),
            device_id_type=MESH,
        )

    for h in range(2):
        sibcopy(1, h).wait_recv()
    for k in range(2):
        product(1, k)
        ccopy(1, k).start()
    acopy(far, 0, True, 4).wait_recv()
    sibcopy(2, 0).start()
    acopy(far, 1, False, 5).wait_recv()
    sibcopy(2, 1).start()
    for h in range(2):
        sibcopy(3, h).wait_recv()
    for k in range(2):
        product(3, k)
        ccopy(3, k).start()

    def xcopy(o, d, k):
        return pltpu.make_async_remote_copy(
            src_ref=qbuf.at[o, k],
            dst_ref=rsum.at[x, k],
            send_sem=x_send.at[d, k],
            recv_sem=x_recv.at[d, k],
            device_id=dev(o, c, y, z),
            device_id_type=MESH,
        )

    def pass_on(o, k):
        for d in range(1, NX):
            @pl.when(o == xpeer(d))
            def _():
                xcopy(xpeer(d), d, k).start()

        @pl.when(o == x)
        def _():
            rsum[x, k] = qbuf[o, k]

    for d in (0, 2):
        for h in range(2):
            sibcopy(d, h).wait_recv()
    for k in range(2):
        product(2, k)
        ccopy(2, k).start()
    for k in range(2):
        product(0, k)
        qbuf[y, k] = pbuf[k, pl.ds(pl.multiple_of(y * TOK, TOK), TOK), :]
        pass_on(y, k)
    @pl.when(x != y)
    def _():
        for k in range(PIECES):
            flip(k).wait_send()

    for h in halos:
        h.wait_send()
    for n in range(PIECES * STEPS):
        for right in (True, False):
            if w_goes(n, right):
                wcopy(n, right).wait_send()
    for cp in to_mode + to_rows + to_back:
        cp.wait_send()
    for h in range(2):
        acopy(y, h, True, h).wait_send()
        acopy(y, h, False, 2 + h).wait_send()
    acopy(lhs, 0, True, 4).wait_send()
    acopy(rhs, 1, False, 5).wait_send()
    for d in range(NY):
        for h in range(2):
            sibcopy(d, h).wait_send()

    for k in range(2):
        for d in (3, 1, 2):
            ccopy(d, k).wait_recv()
            pass_on(ypeer(NY - d), k)
    for k in range(2):
        for d in range(1, NX):
            xcopy(xpeer(d), d, k).wait_recv()
        total = tree([rsum[i, k].astype(F32) for i in range(NX)])
        out_ref[:, k * WIDE : (k + 1) * WIDE] = total.astype(BF16)

    for d in range(1, NY):
        for k in range(2):
            ccopy(d, k).wait_send()
    for d in range(1, NX):
        for k in range(2):
            xcopy(xpeer(d), d, k).wait_send()


def local(
    query_rows, key_rows, value_rows, short_filter, decay_rate, residues, out_weight, record_starts
):
    vmem = pl.BlockSpec(memory_space=pltpu.VMEM)
    hbm = pl.BlockSpec(memory_space=pl.ANY)
    smem = pl.BlockSpec(memory_space=pltpu.SMEM)
    tokens = pltpu.VMEM((TOK * G, 128), F32)
    longer = pltpu.VMEM(((TOK + 2) * G, 128), F32)
    table = pltpu.VMEM((MODES * G, 128), F32)
    dma = pltpu.SemaphoreType.DMA
    return pl.pallas_call(
        kernel,
        out_shape=jax.ShapeDtypeStruct((TOK, COLS), BF16),
        in_specs=[hbm] * 7 + [smem],
        out_specs=vmem,
        scratch_shapes=[
            pltpu.VMEM((TOK, CH), BF16), pltpu.VMEM((TOK, CH), BF16), pltpu.VMEM((TOK, CH), BF16),
            pltpu.VMEM((3, KS, CH), F32), pltpu.VMEM((MODES, CH), F32), pltpu.VMEM((MODES, CH), F32),
            longer, longer, longer, tokens, tokens, tokens,
            pltpu.VMEM((9 * G, 128), F32), table, table, table, table,
            table, table, table, pltpu.VMEM((G, 128), F32), pltpu.VMEM((NY * G, 128), F32),
            pltpu.VMEM((G, 128), F32), table,
            pltpu.VMEM((NZ * TOK, COLS), BF16),
            pltpu.VMEM((NC, NY * TOK, CH), BF16),
            pltpu.VMEM((2, NY * TOK, WIDE), BF16),
            pltpu.VMEM((NY, 2, TOK, WIDE), BF16),
            pltpu.VMEM((NX, 2, TOK, WIDE), BF16),
            dma((6,)), dma((3,)), dma((3,)), dma((2, PIECES)), dma((1,)), dma((2, 32)), dma((2, 32)),
            dma((NZ,)), dma((NZ,)), dma((NY,)), dma((NY,)), dma((NZ,)), dma((NZ,)),
            dma((6,)), dma((6,)), dma((NY, 2)), dma((NY, 2)),
            dma((NY, 2)), dma((NY, 2)), dma((NX, 2)), dma((NX, 2)),
        ],
        compiler_params=pltpu.CompilerParams(
            collective_id=0, has_side_effects=True, vmem_limit_bytes=60 * 1024 * 1024
        ),
    )(
        query_rows, key_rows, value_rows, short_filter,
        decay_rate.T, residues.T, out_weight, record_starts,
    )


def solution(mesh):
    return jax.shard_map(
        local,
        mesh=mesh,
        in_specs=(
            P("ctx", "ch"),
            P("ctx", "ch"),
            P("ctx", "ch"),
            P(None, None, "ch"),
            P("ch", None),
            P("ch", None),
            P("ctx", "ch"),
            P(),
        ),
        out_specs=P("ctx", "ch"),
        check_vma=False,
    )
```
